32 devices in a mesh: poles: 2 (over x), row: 8 (over z, y), col: 2 (over core).
Axes of the slice: x: 2, y: 2, z: 4, core: 2. Of those that a mesh axis runs over, the one named last changes fastest.
Arguments:
- root_inverse: bfloat16 [16384, 8192], P(('poles', 'row'), 'col'), parts along dimension 0, may hold values from -6 to 6
- panels: bfloat16 [4, 1024, 8192], P(('poles', 'col'), None, 'row'), parts along dimension 0, may hold values from -0.1875 to 0.1875
- diag_inverse: bfloat16 [4, 8192, 8192], P(('poles', 'col'), 'row'), parts along dimension 0, may hold values from -6 to 6
- row_lists: int32 [2, 1024], replicated, may hold values from 0 to 8191, as said below
Outputs:
- offdiag_inverse: bfloat16 [4, 1024, 8192], P(('poles', 'col'), None, 'row'), parts along dimension 0
- diag_result: bfloat16 [4, 8192, 8192], P(('poles', 'col'), 'row'), parts along dimension 0
The draws below stay inside these ranges and needn't reach their ends.
There are 2 independent parts, one for each index of `poles`. The reference program is written for one: setup_inputs(seed, part) draws one part's arguments, and reference() takes and returns one part's arrays. A program takes and returns all parts, laid end to end along the dimension named above; an argument that names none is the same for every part. Nothing has to cross between parts.
Inputs may be any that keep to these rules, and one draw needn't show every extreme that they name: `row_lists`: each child's list is strictly increasing and holds the first and the last root row. In each aligned run of 1024 root rows at most 256 of one child's indices fall, and exactly 256 in one run of every list.
All inputs are finite; a program needn't handle non-finite values.
Results may differ from the reference program's by a relative error of at most 0.0055.
Values may be sent and summed in bfloat16 or wider, within the bound.
A program may use at most 192 MiB of HBM per device.

```python
import jax
import jax.numpy as jnp
from jax import lax

NR = 8192
NC = 8192
KC = 1024
N_ROW = 8


def pin_rank(ranks, block, spot):
    line = ranks[block]
    old = line[spot]
    line = jnp.where(line == 0, old, line)
    line = line.at[spot].set(0)
    return ranks.at[block].set(line)


def single_list(key):
    block_rows = NR // N_ROW
    most = 2 * KC // N_ROW
    second = 3 * KC // (2 * N_ROW)
    remain = KC - most - second
    base_count = remain // (N_ROW - 2)
    extra_count = remain % (N_ROW - 2)
    first_key, second_key = jax.random.split(key)
    order = jax.random.permutation(first_key, N_ROW).astype(jnp.int32)
    place = jnp.zeros((N_ROW,), jnp.int32).at[order].set(jnp.arange(N_ROW, dtype=jnp.int32))
    filler = base_count + (place - 2 < extra_count).astype(jnp.int32)
    counts = jnp.where(place == 0, most, jnp.where(place == 1, second, filler))
    block_keys = jax.random.split(second_key, N_ROW)
    ranks = jax.vmap(lambda one_key: jax.random.permutation(one_key, block_rows))(block_keys).astype(jnp.int32)
    ranks = pin_rank(ranks, 0, 0)
    ranks = pin_rank(ranks, N_ROW - 1, block_rows - 1)
    chosen = (ranks < counts[:, None]).reshape(-1)
    picked = jnp.nonzero(chosen, size=KC, fill_value=0)[0]
    return picked.astype(jnp.int32)


def draw_row_lists(key, part):
    first = single_list(jax.random.fold_in(key, 11))
    second = single_list(jax.random.fold_in(key, 23))
    return jnp.stack([first, second])


def block_scale(rng, shape, cuts, smallest, top_value):
    gain = 1.0
    for axis_at, blocks in cuts:
        heights = jax.random.uniform(jax.random.fold_in(jax.random.fold_in(rng, 6), axis_at), (blocks,), jnp.float32, smallest / len(cuts), top_value / len(cuts))
        gain = gain * jnp.repeat(jnp.exp(heights), shape[axis_at] // blocks).reshape((-1,) + (1,) * (len(shape) - 1 - axis_at))
    return gain


def normal_values(stream_key, shape, scale, reach, cuts=(), held_as=jnp.bfloat16):
    array = jax.random.normal(stream_key, shape, jnp.float32) * scale
    if len(cuts) > 0:
        array = block_scale(stream_key, shape, cuts, -0.22, 0.18) * array
    return jnp.clip(array, min=-reach, max=reach).astype(held_as)


def setup_inputs(seed: int = 0, part: int = 0) -> dict:
    streams_of = jax.random.split(jax.random.key(seed), 5)
    own_keys = jax.random.split(jax.random.fold_in(streams_of[4], part), 5)
    return {
        "root_inverse": normal_values(own_keys[0], (NR, NR), 1.0, 6.0, ((0, 8), (1, 2))),
        "panels": normal_values(own_keys[1], (2, KC, NC), KC ** -0.5, 0.1875, ((0, 2), (2, 8))),
        "diag_inverse": normal_values(own_keys[2], (2, NC, NC), 1.0, 6.0, ((0, 2), (1, 8))),
        "row_lists": draw_row_lists(jax.random.fold_in(streams_of[4], 71), part),
    }


def wide_dot(left, right):
    return jnp.dot(left.astype(jnp.float32), right.astype(jnp.float32), precision=lax.Precision.HIGHEST)


def one_child(root_inverse, panel, diag_block, rows):
    root_part = jnp.take(jnp.take(root_inverse, rows, axis=0), rows, axis=1)
    offdiag = (-wide_dot(root_part, panel)).astype(jnp.bfloat16)
    update = wide_dot(offdiag.T, panel)
    block = (diag_block.astype(jnp.float32) - update).astype(jnp.bfloat16)
    block = lax.optimization_barrier(block)
    wide = block.astype(jnp.float32)
    result = ((wide + wide.T) * 0.5).astype(jnp.bfloat16)
    return offdiag, result


def reference(root_inverse, panels, diag_inverse, row_lists):
    first_off, first_diag = one_child(root_inverse, panels[0], diag_inverse[0], row_lists[0].astype(jnp.int32))
    second_off, second_diag = one_child(root_inverse, panels[1], diag_inverse[1], row_lists[1].astype(jnp.int32))
    return jnp.stack([first_off, second_off]), jnp.stack([first_diag, second_diag])
```

```python
import functools

import jax
import jax.numpy as jnp
from jax import lax
from jax.experimental import pallas as pl
from jax.experimental.pallas import tpu as pltpu
from jax.sharding import PartitionSpec as P

MESH = pl.DeviceIdType.MESH
F32 = jnp.float32
BF16 = jnp.bfloat16


def flip(row, mask):
    bit = 1
    while bit <= mask:
        if mask & bit:
            row = row + bit - 2 * bit * ((row // bit) % 2)
        bit *= 2
    return row


def tile_of(size, most):
    return most if size % most == 0 else size


def exchange_kernel(
    n, root_ref, panel_ref, diag_ref, sel_ref, cols_ref, place_ref,
    off_ref, mine_ref, theirs_ref,
    root_v, picks, other_pick, listed, root_part, root_part_t, wide_t, p_all, d_buf,
    local_sem, copy_sem, x_sem, p_send, p_recv, g_send, g_recv, d_send, d_recv,
):
    half = n // 2
    row = lax.axis_index("row")
    col = lax.axis_index("col")
    side = row // half
    computes = (side + col) % 2 == 1
    keeps = (side + col) % 2 == 0
    block = panel_ref.shape[2]
    depth = panel_ref.shape[1]
    most = picks.shape[1]
    peers = [flip(row, m) for m in range(n)]

    def diag_block(m):
        start = pl.multiple_of(peers[m] * block, block)
        return diag_ref.at[0, :, pl.ds(start, block)]

    root_copy = pltpu.make_async_copy(root_ref, root_v, local_sem.at[0])
    root_copy.start()
    panel_copy = pltpu.make_async_copy(panel_ref.at[0], p_all.at[0], local_sem.at[1])
    panel_copy.start()
    own_copy = pltpu.make_async_copy(diag_block(0), theirs_ref.at[0], copy_sem.at[0])
    own_copy.start()

    barrier = pltpu.get_barrier_semaphore()
    for m in range(1, n):
        pl.semaphore_signal(barrier, inc=1, device_id={"row": peers[m]}, device_id_type=MESH)
    pl.semaphore_signal(barrier, inc=1, device_id={"col": 1 - col}, device_id_type=MESH)
    pl.semaphore_wait(barrier, n)

    def remote(src, dst, send, recv, mask):
        return pltpu.make_async_remote_copy(
            src_ref=src, dst_ref=dst, send_sem=send, recv_sem=recv,
            device_id={"row": peers[mask]}, device_id_type=MESH,
        )

    def spread(buf, send, recv, base):
        held, steps, bit = [base], [], half // 2
        while bit >= 1:
            steps.append([
                remote(buf.at[m], buf.at[m ^ bit], send.at[base + len(held) - 1 + i],
                       recv.at[m ^ bit], bit)
                for i, m in enumerate(held)
            ])
            held = held + [m ^ bit for m in held]
            bit //= 2
        return steps

    def cross(buf, send, recv):
        return remote(buf.at[0], buf.at[half], send.at[n - 1], recv.at[half], half)

    def send_diag(m):
        return remote(diag_block(m), theirs_ref.at[m], d_send.at[m], d_recv.at[m], m)

    def send_mine(m):
        return remote(mine_ref.at[m], theirs_ref.at[m], d_send.at[m], d_recv.at[m], m)

    p_own, p_far = spread(p_all, p_send, p_recv, 0), spread(p_all, p_send, p_recv, half)
    g_own, g_far = spread(listed, g_send, g_recv, 0), spread(listed, g_send, g_recv, half)
    p_cross, g_cross = cross(p_all, p_send, p_recv), cross(listed, g_send, g_recv)

    panel_copy.wait()

    @pl.when(keeps)
    def _():
        p_cross.start()

    if p_own:
        p_own[0][0].start()

    root_copy.wait()
    block_rows, half_cols = root_v.shape
    width = tile_of(half_cols, 512)
    row_ids = lax.broadcasted_iota(jnp.int32, (2 * most, block_rows), 1)
    take_rows = jnp.where(sel_ref[...] == row_ids, 1.0, 0.0).astype(BF16)

    def pick_tile(t, carry):
        own, far = carry
        at = pl.multiple_of(t * width, width)
        taken = jnp.dot(take_rows, root_v[:, pl.ds(at, width)], preferred_element_type=F32).astype(BF16)
        col_ids = lax.broadcasted_iota(jnp.int32, (width, depth), 0) + t * width
        take_own = jnp.where(cols_ref[0:1, :] == col_ids, 1.0, 0.0).astype(BF16)
        take_far = jnp.where(cols_ref[1:2, :] == col_ids, 1.0, 0.0).astype(BF16)
        own = own + jnp.dot(taken[:most], take_own, preferred_element_type=F32)
        far = far + jnp.dot(taken[most:], take_far, preferred_element_type=F32)
        return own, far

    zero = jnp.zeros((most, depth), F32)
    own, far = lax.fori_loop(0, half_cols // width, pick_tile, (zero, zero))
    picks[1] = far.astype(BF16)
    picks[0] = own.astype(BF16)
    over = pltpu.make_async_remote_copy(
        src_ref=picks.at[1], dst_ref=other_pick, send_sem=x_sem.at[0], recv_sem=x_sem.at[1],
        device_id={"col": 1 - col}, device_id_type=MESH,
    )
    over.start()
    over.wait()
    listed[0] = (picks[0].astype(F32) + other_pick[...].astype(F32)).astype(BF16)
    g_cross.start()
    if g_own:
        g_own[0][0].start()

    @pl.when(keeps)
    def _():
        for m in range(half, n):
            send_diag(m).start()
        for m in range(half, n):
            pltpu.make_async_copy(diag_block(m), mine_ref.at[m], copy_sem.at[m]).start()

    @pl.when(computes)
    def _():
        for m in range(1, half):
            send_diag(m).start()

    def finish(steps, k):
        for copy in steps[k]:
            copy.wait_recv()

    def begin(steps, k):
        if k < len(steps):
            for copy in steps[k]:
                copy.start()

    levels = len(p_own)
    for k in range(levels):
        finish(g_own, k)
        begin(g_own, k + 1)
        if k == 0:
            g_cross.wait_recv()
        else:
            finish(g_far, k - 1)
        begin(g_far, k)
        finish(p_own, k)
        begin(p_own, k + 1)

        @pl.when(computes)
        def _():
            if k == 0:
                p_cross.wait_recv()
            else:
                finish(p_far, k - 1)
            begin(p_far, k)

    if levels:
        finish(g_far, levels - 1)
    else:
        g_cross.wait_recv()

        @pl.when(computes)
        def _():
            p_cross.wait_recv()

    @pl.when(keeps)
    def _():
        for m in range(1, half):
            send_diag(m).start()

    rows_step = tile_of(depth, 256)
    slots = listed.shape[0] * most
    all_listed = listed[...].reshape(slots, depth)

    def put_rows(t, carry):
        at = pl.multiple_of(t * rows_step, rows_step)
        ids = lax.broadcasted_iota(jnp.int32, (rows_step, slots), 1)
        put = jnp.where(place_ref[pl.ds(at, rows_step), :] == ids, 1.0, 0.0).astype(BF16)
        root_part[pl.ds(at, rows_step), :] = jnp.dot(put, all_listed, preferred_element_type=F32).astype(BF16)
        return carry

    lax.fori_loop(0, depth // rows_step, put_rows, 0)

    def turn(t, carry):
        at = pl.multiple_of(t * rows_step, rows_step)
        root_part_t[:, pl.ds(at, rows_step)] = root_part[pl.ds(at, rows_step), :].astype(F32).T.astype(BF16)
        return carry

    lax.fori_loop(0, depth // rows_step, turn, 0)
    cols_step = tile_of(block, 256)

    def products(t, carry):
        at = pl.multiple_of(t * cols_step, cols_step)
        panel = p_all[0, :, pl.ds(at, cols_step)]
        plain = jnp.dot(root_part[...], panel, preferred_element_type=F32)
        turned = jnp.dot(root_part_t[...], panel, preferred_element_type=F32)
        off_ref[0, :, pl.ds(at, cols_step)] = (-plain).astype(BF16)
        wide_t[pl.ds(at, cols_step), :] = (plain + turned).T.astype(BF16)
        return carry

    lax.fori_loop(0, block // cols_step, products, 0)

    def update(m):
        load = pltpu.make_async_copy(diag_block(m), d_buf, local_sem.at[0])
        load.start()
        load.wait()

        def one(t, carry):
            at = pl.multiple_of(t * cols_step, cols_step)
            part = jnp.dot(wide_t[pl.ds(at, cols_step), :], p_all[m], preferred_element_type=F32)
            d_buf[pl.ds(at, cols_step), :] = (d_buf[pl.ds(at, cols_step), :].astype(F32) + part).astype(BF16)
            return carry

        lax.fori_loop(0, block // cols_step, one, 0)
        store = pltpu.make_async_copy(d_buf, mine_ref.at[m], local_sem.at[1])
        store.start()
        store.wait()

    @pl.when(computes)
    def _():
        for m in range(half, n):
            if levels and m == half + 1:
                finish(p_far, levels - 1)
            update(m)
            send_mine(m).start()

    for m in range(half):
        update(m)

    own_copy.wait()

    @pl.when(keeps)
    def _():
        p_cross.wait_send()
        for m in range(half, n):
            pltpu.make_async_copy(diag_block(m), mine_ref.at[m], copy_sem.at[m]).wait()
            send_diag(m).wait()

    @pl.when(computes)
    def _():
        for step in p_far:
            for copy in step:
                copy.wait_send()
        for m in range(half, n):
            send_mine(m).wait()

    g_cross.wait_send()
    for steps in (p_own, g_own, g_far):
        for step in steps:
            for copy in step:
                copy.wait_send()
    for m in range(1, half):
        send_diag(m).wait()


def symmetrize_kernel(row_ref, mine_ref, theirs_ref, out_ref):
    out_ref[0] = ((mine_ref[0].astype(F32) + theirs_ref[0].astype(F32).T) * 0.5).astype(BF16)


def per_device(root_inverse, panels, diag_inverse, row_lists):
    row = lax.axis_index("row")
    col = lax.axis_index("col")
    n = lax.axis_size("row")
    listed = row_lists.shape[1]
    most = 2 * listed // n
    block_rows, half_cols = root_inverse.shape
    block = panels.shape[2]

    own_rows = jnp.where(col == 0, row_lists[0], row_lists[1])
    far_rows = jnp.where(col == 0, row_lists[1], row_lists[0])
    both = jnp.stack([own_rows, far_rows])
    lower = row * block_rows
    inside = (both >= lower) & (both < lower + block_rows)
    spot = jnp.arange(listed, dtype=jnp.int32)
    first = jnp.sum((both < lower).astype(jnp.int32), axis=1, keepdims=True)
    rank = jnp.where(inside, spot[None] - first, -1)
    slots = jnp.arange(most, dtype=jnp.int32)
    hit = rank[:, None, :] == slots[None, :, None]
    sel = jnp.max(jnp.where(hit, both[:, None, :] - lower, -1), axis=2).reshape(2 * most, 1)
    cols = both - col * half_cols
    owner = own_rows // block_rows
    start = jnp.sum((own_rows[None, :] < (owner * block_rows)[:, None]).astype(jnp.int32), axis=1)
    place = (jnp.bitwise_xor(owner, row) * most + spot - start).reshape(listed, 1)

    hbm = pl.BlockSpec(memory_space=pl.ANY)
    vmem = pl.BlockSpec(memory_space=pltpu.VMEM)
    dma = pltpu.SemaphoreType.DMA
    off, mine, theirs = pl.pallas_call(
        functools.partial(exchange_kernel, n),
        out_shape=(
            jax.ShapeDtypeStruct(panels.shape, BF16),
            jax.ShapeDtypeStruct((n, block, block), BF16),
            jax.ShapeDtypeStruct((n, block, block), BF16),
        ),
        in_specs=[hbm, hbm, hbm, vmem, vmem, vmem],
        out_specs=(vmem, hbm, hbm),
        scratch_shapes=[
            pltpu.VMEM((block_rows, half_cols), BF16),
            pltpu.VMEM((2, most, listed), BF16),
            pltpu.VMEM((most, listed), BF16),
            pltpu.VMEM((n, most, listed), BF16),
            pltpu.VMEM((listed, listed), BF16),
            pltpu.VMEM((listed, listed), BF16),
            pltpu.VMEM((block, listed), BF16),
            pltpu.VMEM((n, listed, block), BF16),
            pltpu.VMEM((block, block), BF16),
            dma((2,)), dma((n,)), dma((2,)),
            dma((n,)), dma((n,)), dma((n,)), dma((n,)), dma((n,)), dma((n,)),
        ],
        compiler_params=pltpu.CompilerParams(
            collective_id=0, has_side_effects=True, vmem_limit_bytes=60 * 2**20
        ),
        name="exchange",
    )(root_inverse, panels, diag_inverse, sel, cols, place)

    strip = tile_of(block, 256)
    result = pl.pallas_call(
        symmetrize_kernel,
        grid_spec=pltpu.PrefetchScalarGridSpec(
            num_scalar_prefetch=1,
            grid=(n, block // strip),
            in_specs=[
                pl.BlockSpec((1, strip, block), lambda m, t, at: (m, t, 0)),
                pl.BlockSpec((1, block, strip), lambda m, t, at: (m, 0, t)),
            ],
            out_specs=pl.BlockSpec((1, strip, block), lambda m, t, at: (0, t, m ^ at[0])),
        ),
        out_shape=jax.ShapeDtypeStruct(diag_inverse.shape, BF16),
        compiler_params=pltpu.CompilerParams(vmem_limit_bytes=32 * 2**20),
        name="symmetrize",
    )(row.reshape(1), mine, theirs)
    return (off, result)


def solution(mesh):
    placed = (
        P(("poles", "row"), "col"),
        P(("poles", "col"), None, "row"),
        P(("poles", "col"), "row", None),
        P(),
    )
    return jax.shard_map(
        per_device,
        mesh=mesh,
        in_specs=placed,
        out_specs=(P(("poles", "col"), None, "row"), P(("poles", "col"), "row", None)),
        check_vma=False,
    )
```

```python
import functools

import jax
import jax.numpy as jnp
from jax import lax
from jax.experimental import pallas as pl
from jax.experimental.pallas import tpu as pltpu
from jax.sharding import PartitionSpec as P

MESH = pl.DeviceIdType.MESH
F32 = jnp.float32
BF16 = jnp.bfloat16


def flip(row, mask):
    bit = 1
    while bit <= mask:
        if mask & bit:
            row = row + bit - 2 * bit * ((row // bit) % 2)
        bit *= 2
    return row


def tile_of(size, most):
    return most if size % most == 0 else size


def exchange_kernel(
    n, root_ref, panel_ref, diag_ref, sel_ref, cols_ref, place_ref,
    off_ref, mine_ref, theirs_ref,
    root_v, picks, other_pick, listed, root_part, root_part_t, wide_t, p_all, d_buf,
    local_sem, copy_sem, x_sem, p_send, p_recv, g_send, g_recv, d_send, d_recv,
):
    half = n // 2
    row = lax.axis_index("row")
    col = lax.axis_index("col")
    side = row // half
    computes = (side + col) % 2 == 1
    keeps = (side + col) % 2 == 0
    block = panel_ref.shape[2]
    depth = panel_ref.shape[1]
    most = picks.shape[1]
    peers = [flip(row, m) for m in range(n)]

    def diag_block(m):
        start = pl.multiple_of(peers[m] * block, block)
        return diag_ref.at[0, :, pl.ds(start, block)]

    root_copy = pltpu.make_async_copy(root_ref, root_v, local_sem.at[0])
    root_copy.start()
    panel_copy = pltpu.make_async_copy(panel_ref.at[0], p_all.at[0], local_sem.at[1])
    panel_copy.start()
    own_copy = pltpu.make_async_copy(diag_block(0), theirs_ref.at[0], copy_sem.at[0])
    own_copy.start()

    barrier = pltpu.get_barrier_semaphore()
    for m in range(1, n):
        pl.semaphore_signal(barrier, inc=1, device_id={"row": peers[m]}, device_id_type=MESH)
    pl.semaphore_signal(barrier, inc=1, device_id={"col": 1 - col}, device_id_type=MESH)
    pl.semaphore_wait(barrier, n)

    def remote(src, dst, send, recv, mask):
        return pltpu.make_async_remote_copy(
            src_ref=src, dst_ref=dst, send_sem=send, recv_sem=recv,
            device_id={"row": peers[mask]}, device_id_type=MESH,
        )

    pieces = p_send.shape[1]
    piece = depth // pieces

    def panel_copy_to(source, slot, send, mask, c):
        rows = pl.ds(c * piece, piece)
        return remote(p_all.at[source, rows], p_all.at[slot, rows],
                      p_send.at[send, c], p_recv.at[slot, c], mask)

    def spread(base):
        held, steps, bit = [base], [], half // 2
        while bit >= 1:
            steps.append([
                [panel_copy_to(m, m ^ bit, base + len(held) - 1 + i, bit, c) for i, m in enumerate(held)]
                for c in range(pieces)
            ])
            held = held + [m ^ bit for m in held]
            bit //= 2
        return steps

    def send_diag(m):
        return remote(diag_block(m), theirs_ref.at[m], d_send.at[m], d_recv.at[m], m)

    def send_mine(m):
        return remote(mine_ref.at[m], theirs_ref.at[m], d_send.at[m], d_recv.at[m], m)

    p_own, p_far = spread(0), spread(half)
    p_cross = [panel_copy_to(0, half, n - 1, half, c) for c in range(pieces)]
    g_cross = remote(listed.at[0], listed.at[half], g_send.at[half], g_recv.at[half], half)
    g_own = [remote(listed.at[0], listed.at[m], g_send.at[m], g_recv.at[m], m) for m in range(1, half)]
    g_far = [
        remote(listed.at[half], listed.at[m], g_send.at[m], g_recv.at[m], m - half)
        for m in range(half + 1, n)
    ]

    panel_copy.wait()

    @pl.when(keeps)
    def _():
        for copy in p_cross:
            copy.start()

    root_copy.wait()
    block_rows, half_cols = root_v.shape
    width = tile_of(half_cols, 512)
    row_ids = lax.broadcasted_iota(jnp.int32, (2 * most, block_rows), 1)
    take_rows = jnp.where(sel_ref[...] == row_ids, 1.0, 0.0).astype(BF16)

    def pick_tile(t, carry):
        own, far = carry
        at = pl.multiple_of(t * width, width)
        taken = jnp.dot(take_rows, root_v[:, pl.ds(at, width)], preferred_element_type=F32).astype(BF16)
        col_ids = lax.broadcasted_iota(jnp.int32, (width, depth), 0) + t * width
        take_own = jnp.where(cols_ref[0:1, :] == col_ids, 1.0, 0.0).astype(BF16)
        take_far = jnp.where(cols_ref[1:2, :] == col_ids, 1.0, 0.0).astype(BF16)
        own = own + jnp.dot(taken[:most], take_own, preferred_element_type=F32)
        far = far + jnp.dot(taken[most:], take_far, preferred_element_type=F32)
        return own, far

    zero = jnp.zeros((most, depth), F32)
    own, far = lax.fori_loop(0, half_cols // width, pick_tile, (zero, zero))
    picks[1] = far.astype(BF16)
    picks[0] = own.astype(BF16)
    over = pltpu.make_async_remote_copy(
        src_ref=picks.at[1], dst_ref=other_pick, send_sem=x_sem.at[0], recv_sem=x_sem.at[1],
        device_id={"col": 1 - col}, device_id_type=MESH,
    )
    over.start()
    over.wait()
    listed[0] = (picks[0].astype(F32) + other_pick[...].astype(F32)).astype(BF16)
    g_cross.start()
    for copy in g_own:
        copy.start()

    @pl.when(keeps)
    def _():
        for m in range(half, n):
            send_diag(m).start()
        for m in range(half, n):
            pltpu.make_async_copy(diag_block(m), mine_ref.at[m], copy_sem.at[m]).start()

    def finish(steps, k, c):
        for copy in steps[k][c]:
            copy.wait_recv()

    def begin(steps, k, c):
        if k < len(steps):
            for copy in steps[k][c]:
                copy.start()

    levels = len(p_own)
    g_cross.wait_recv()
    for copy in g_far:
        copy.start()

    @pl.when(computes)
    def _():
        for c in range(pieces):
            p_cross[c].wait_recv()
            begin(p_far, 0, c)
        for k in range(levels - 1):
            for c in range(pieces):
                finish(p_far, k, c)
                begin(p_far, k + 1, c)

    for copy in g_own + g_far:
        copy.wait_recv()

    for c in range(pieces):
        begin(p_own, 0, c)
    for m in range(1, half):
        send_diag(m).start()

    rows_step = tile_of(depth, 256)
    slots = listed.shape[0] * most
    all_listed = listed[...].reshape(slots, depth)

    def put_rows(t, carry):
        at = pl.multiple_of(t * rows_step, rows_step)
        ids = lax.broadcasted_iota(jnp.int32, (rows_step, slots), 1)
        put = jnp.where(place_ref[pl.ds(at, rows_step), :] == ids, 1.0, 0.0).astype(BF16)
        root_part[pl.ds(at, rows_step), :] = jnp.dot(put, all_listed, preferred_element_type=F32).astype(BF16)
        return carry

    lax.fori_loop(0, depth // rows_step, put_rows, 0)

    def turn(t, carry):
        at = pl.multiple_of(t * rows_step, rows_step)
        root_part_t[:, pl.ds(at, rows_step)] = root_part[pl.ds(at, rows_step), :].astype(F32).T.astype(BF16)
        return carry

    lax.fori_loop(0, depth // rows_step, turn, 0)
    cols_step = tile_of(block, 256)

    def products(t, carry):
        at = pl.multiple_of(t * cols_step, cols_step)
        panel = p_all[0, :, pl.ds(at, cols_step)]
        plain = jnp.dot(root_part[...], panel, preferred_element_type=F32)
        turned = jnp.dot(root_part_t[...], panel, preferred_element_type=F32)
        off_ref[0, :, pl.ds(at, cols_step)] = (-plain).astype(BF16)
        wide_t[pl.ds(at, cols_step), :] = (plain + turned).T.astype(BF16)
        return carry

    lax.fori_loop(0, block // cols_step, products, 0)

    def update(m):
        load = pltpu.make_async_copy(diag_block(m), d_buf, local_sem.at[0])
        load.start()
        load.wait()

        def one(t, carry):
            at = pl.multiple_of(t * cols_step, cols_step)
            part = jnp.dot(wide_t[pl.ds(at, cols_step), :], p_all[m], preferred_element_type=F32)
            d_buf[pl.ds(at, cols_step), :] = (d_buf[pl.ds(at, cols_step), :].astype(F32) + part).astype(BF16)
            return carry

        lax.fori_loop(0, block // cols_step, one, 0)
        store = pltpu.make_async_copy(d_buf, mine_ref.at[m], local_sem.at[1])
        store.start()
        store.wait()

    @pl.when(computes)
    def _():
        update(half)
        send_mine(half).start()
        arrived = [half]
        for k in range(levels):
            if k == levels - 1:
                for c in range(pieces):
                    finish(p_far, k, c)
            fresh = [m ^ (half >> (k + 1)) for m in arrived]
            for m in fresh:
                update(m)
                send_mine(m).start()
            arrived = arrived + fresh

    update(0)
    arrived = [0]
    for k in range(levels):
        for c in range(pieces):
            finish(p_own, k, c)
            begin(p_own, k + 1, c)
        fresh = [m ^ (half >> (k + 1)) for m in arrived]
        for m in fresh:
            update(m)
        arrived = arrived + fresh

    own_copy.wait()

    @pl.when(keeps)
    def _():
        for copy in p_cross:
            copy.wait_send()
        for m in range(half, n):
            pltpu.make_async_copy(diag_block(m), mine_ref.at[m], copy_sem.at[m]).wait()
            send_diag(m).wait()

    @pl.when(computes)
    def _():
        for step in p_far:
            for copies in step:
                for copy in copies:
                    copy.wait_send()
        for m in range(half, n):
            send_mine(m).wait()

    for copy in [g_cross] + g_own + g_far:
        copy.wait_send()
    for step in p_own:
        for copies in step:
            for copy in copies:
                copy.wait_send()
    for m in range(1, half):
        send_diag(m).wait()


def symmetrize_kernel(row_ref, mine_ref, theirs_ref, out_ref):
    out_ref[0] = ((mine_ref[0].astype(F32) + theirs_ref[0].T.astype(F32)) * 0.5).astype(BF16)


def per_device(root_inverse, panels, diag_inverse, row_lists):
    row = lax.axis_index("row")
    col = lax.axis_index("col")
    n = lax.axis_size("row")
    listed = row_lists.shape[1]
    most = 2 * listed // n
    block_rows, half_cols = root_inverse.shape
    block = panels.shape[2]

    own_rows = jnp.where(col == 0, row_lists[0], row_lists[1])
    far_rows = jnp.where(col == 0, row_lists[1], row_lists[0])
    both = jnp.stack([own_rows, far_rows])
    lower = row * block_rows
    inside = (both >= lower) & (both < lower + block_rows)
    spot = jnp.arange(listed, dtype=jnp.int32)
    first = jnp.sum((both < lower).astype(jnp.int32), axis=1, keepdims=True)
    rank = jnp.where(inside, spot[None] - first, -1)
    slots = jnp.arange(most, dtype=jnp.int32)
    hit = rank[:, None, :] == slots[None, :, None]
    sel = jnp.max(jnp.where(hit, both[:, None, :] - lower, -1), axis=2).reshape(2 * most, 1)
    cols = both - col * half_cols
    owner = own_rows // block_rows
    start = jnp.sum((own_rows[None, :] < (owner * block_rows)[:, None]).astype(jnp.int32), axis=1)
    place = (jnp.bitwise_xor(owner, row) * most + spot - start).reshape(listed, 1)

    hbm = pl.BlockSpec(memory_space=pl.ANY)
    vmem = pl.BlockSpec(memory_space=pltpu.VMEM)
    dma = pltpu.SemaphoreType.DMA
    off, mine, theirs = pl.pallas_call(
        functools.partial(exchange_kernel, n),
        out_shape=(
            jax.ShapeDtypeStruct(panels.shape, BF16),
            jax.ShapeDtypeStruct((n, block, block), BF16),
            jax.ShapeDtypeStruct((n, block, block), BF16),
        ),
        in_specs=[hbm, hbm, hbm, vmem, vmem, vmem],
        out_specs=(vmem, hbm, hbm),
        scratch_shapes=[
            pltpu.VMEM((block_rows, half_cols), BF16),
            pltpu.VMEM((2, most, listed), BF16),
            pltpu.VMEM((most, listed), BF16),
            pltpu.VMEM((n, most, listed), BF16),
            pltpu.VMEM((listed, listed), BF16),
            pltpu.VMEM((listed, listed), BF16),
            pltpu.VMEM((block, listed), BF16),
            pltpu.VMEM((n, listed, block), BF16),
            pltpu.VMEM((block, block), BF16),
            dma((2,)), dma((n,)), dma((2,)),
            dma((n, 4)), dma((n, 4)), dma((n,)), dma((n,)), dma((n,)), dma((n,)),
        ],
        compiler_params=pltpu.CompilerParams(
            collective_id=0, has_side_effects=True, vmem_limit_bytes=60 * 2**20
        ),
        name="exchange",
    )(root_inverse, panels, diag_inverse, sel, cols, place)

    strip = tile_of(block, 512)
    result = pl.pallas_call(
        symmetrize_kernel,
        grid_spec=pltpu.PrefetchScalarGridSpec(
            num_scalar_prefetch=1,
            grid=(n, block // strip),
            in_specs=[
                pl.BlockSpec((1, strip, block), lambda m, t, at: (m, t, 0)),
                pl.BlockSpec((1, block, strip), lambda m, t, at: (m, 0, t)),
            ],
            out_specs=pl.BlockSpec((1, strip, block), lambda m, t, at: (0, t, m ^ at[0])),
        ),
        out_shape=jax.ShapeDtypeStruct(diag_inverse.shape, BF16),
        compiler_params=pltpu.CompilerParams(vmem_limit_bytes=60 * 2**20),
        name="symmetrize",
    )(row.reshape(1), mine, theirs)
    return (off, result)


def solution(mesh):
    placed = (
        P(("poles", "row"), "col"),
        P(("poles", "col"), None, "row"),
        P(("poles", "col"), "row", None),
        P(),
    )
    return jax.shard_map(
        per_device,
        mesh=mesh,
        in_specs=placed,
        out_specs=(P(("poles", "col"), None, "row"), P(("poles", "col"), "row", None)),
        check_vma=False,
    )
```
